32 devices in a mesh: sub: 16 (over z, y, core), col: 2 (over x).
Axes of the slice: x: 2, y: 2, z: 4, core: 2. Of those that a mesh axis runs over, the one named last changes fastest.
Arguments:
- right_sides: float32 [64, 20480], P(None, ('sub', 'col')), may hold values from -6 to 6
- operator: float32 [16, 1536, 1280], P('sub', None, 'col'), may hold values from -0.15625 to 0.15625
- local_inverse: float32 [16, 1536, 1280], P('sub', None, 'col'), may hold values from -0.15625 to 0.15625
- coarse_basis: float32 [16, 1536, 64], P('sub'), may hold values from -0.15625 to 0.15625
- coarse_inverse: float32 [1024, 1024], P('sub', 'col'), may hold values from -0.5 to 0.5
- send_index: int32 [16, 2, 4, 32], P('sub', 'col'), may hold values from 0 to 639
- halo_count: int32 [16, 2, 4], P('sub', 'col'), may hold values from 1 to 32, as said below
Outputs:
- solution: float32 [64, 20480], P(None, ('sub', 'col'))
- residual: float32 [64, 20480], P(None, ('sub', 'col'))
The draws below stay inside these ranges and needn't reach their ends.
Inputs may be any that keep to these rules, and one draw needn't show every extreme that they name: `halo_count`: on every device of every draw at least one of its 4 counts equals 32.
All inputs are finite; a program needn't handle non-finite values.
Results may differ from the reference program's by a relative error of at most 0.000078.
Values sent between devices are 32-bit elements; how exact they have to be, the bound alone decides.
A program may use at most 64 MiB of HBM per device.

```python
import jax
import jax.numpy as jnp
from jax import lax

NRHS = 64
EXT = 1536
MODES = 64
NB = 4
HB = 32
SUBS = 16
CH = 768
OWNC = 640
OWN = 1280
MQ = 32
NC = 1024
STRIDE = 4
N_COL = 2


def draw_halo_count(key, part):
    first_key, second_key = jax.random.split(key)
    counts = jax.random.randint(first_key, (SUBS, N_COL, NB), 1, HB + 1)
    which = jax.random.randint(second_key, (SUBS, N_COL, 1), 0, NB)
    slots = jnp.arange(NB, dtype=jnp.int32)[None, None, :]
    return jnp.where(slots == which, HB, counts).astype(jnp.int32)


def set_ends(entries, stream_key, smallest, high):
    longest = entries.shape.index(max(entries.shape))
    spots = []
    for shift in (0, 1):
        where = [jax.random.randint(jax.random.fold_in(stream_key, axis), (), 0, length) for axis, length in enumerate(entries.shape)]
        where[longest] = (where[longest] + shift) % entries.shape[longest]
        spots.append(tuple(where))
    return entries.at[spots[0]].set(smallest).at[spots[1]].set(high)


def block_levels(rng, dims, cuts, smallest, top_value):
    level = 1.0
    for position, shards_of in cuts:
        steps = jax.random.uniform(jax.random.fold_in(jax.random.fold_in(rng, 6), position), (shards_of,), jnp.float32, smallest / len(cuts), top_value / len(cuts))
        level = level * jnp.repeat(jnp.exp(steps), dims[position] // shards_of).reshape((-1,) + (1,) * (len(dims) - 1 - position))
    return level


def normal_values(stream_key, shape, width, limit, cuts=(), held_as=jnp.bfloat16):
    level = block_levels(stream_key, shape, cuts, -0.22, 0.18) if cuts else 1.0
    array = jax.random.normal(stream_key, shape, jnp.float32) * width * level
    return jnp.minimum(jnp.maximum(array, -limit), limit).astype(held_as)


def setup_inputs(seed: int = 0) -> dict:
    key_list = jax.random.split(jax.random.key(seed), 8)
    right_sides = normal_values(key_list[0], (NRHS, SUBS * OWN), 1.0, 6.0, ((1, 32),), jnp.float32)
    operator = normal_values(key_list[1], (SUBS, EXT, OWN), EXT ** -0.5, 0.15625, ((0, 16), (2, 2)), jnp.float32)
    local_inverse = normal_values(key_list[2], (SUBS, EXT, OWN), EXT ** -0.5, 0.15625, ((0, 16), (2, 2)), jnp.float32)
    coarse_basis = normal_values(key_list[3], (SUBS, EXT, MODES), EXT ** -0.5, 0.15625, ((0, 16),), jnp.float32)
    coarse_inverse = normal_values(key_list[4], (NC, NC), (NC // 8) ** -0.5, 0.5, ((0, 16), (1, 2)), jnp.float32)
    send_index = set_ends(jax.random.randint(key_list[5], (SUBS, N_COL, NB, HB), 0, OWNC), jax.random.fold_in(key_list[5], 1), 0, OWNC - 1).astype(jnp.int32)
    halo_count = draw_halo_count(jax.random.fold_in(key_list[7], 71), 0)
    return dict(right_sides=right_sides, operator=operator, local_inverse=local_inverse, coarse_basis=coarse_basis, coarse_inverse=coarse_inverse, send_index=send_index, halo_count=halo_count)


HIGH = lax.Precision.HIGHEST


def shifted(packed, offset):
    blank_rows = jnp.zeros_like(packed[:, :abs(offset)])
    if offset > 0:
        return jnp.concatenate([blank_rows, packed[:, :-offset]], axis=1)
    return jnp.concatenate([packed[:, -offset:], blank_rows], axis=1)


def extended(field, send_index, halo_count):
    rhs_width = field.shape[0]
    own_rows = field.reshape(rhs_width, SUBS, N_COL, OWNC)
    slots = jnp.arange(HB, dtype=jnp.int32)
    live_slots = (slots[None, None, None, :] < halo_count[:, :, :, None]).astype(jnp.float32)
    pieces = [own_rows]
    for number, offset in enumerate((1, -1, STRIDE, -STRIDE)):
        chosen = jnp.broadcast_to(send_index[None, :, :, number, :], (rhs_width, SUBS, N_COL, HB)).astype(jnp.int32)
        packed = jnp.take_along_axis(own_rows, chosen, axis=3) * live_slots[None, :, :, number, :]
        pieces.append(shifted(packed, offset))
    return jnp.concatenate(pieces, axis=3).reshape(rhs_width, SUBS, EXT)


def precondition(field, local_inverse, coarse_basis, coarse_inverse, send_index, halo_count):
    rhs_width = field.shape[0]
    extension = extended(field, send_index, halo_count)
    local_part = jnp.einsum("rse,seo->rso", extension, local_inverse, precision=HIGH)
    mode_coeffs = jnp.einsum("rse,sem->smr", extension, coarse_basis, precision=HIGH)
    ordered = mode_coeffs.reshape(SUBS, N_COL, MQ, rhs_width).transpose(1, 0, 2, 3).reshape(NC, rhs_width)
    coarse_vals = jnp.dot(coarse_inverse, ordered, precision=HIGH).reshape(SUBS, MODES, rhs_width)
    own_basis = coarse_basis.reshape(SUBS, N_COL, CH, MODES)[:, :, :OWNC].reshape(SUBS, OWN, MODES)
    coarse_part = jnp.einsum("smr,som->rso", coarse_vals, own_basis, precision=HIGH)
    return (local_part + coarse_part).reshape(rhs_width, SUBS * OWN)


def reference(right_sides, operator, local_inverse, coarse_basis, coarse_inverse, send_index, halo_count):
    rhs_width = right_sides.shape[0]
    first_pass = precondition(right_sides, local_inverse, coarse_basis, coarse_inverse, send_index, halo_count)
    extension = extended(first_pass, send_index, halo_count)
    applied = jnp.einsum("rse,seo->rso", extension, operator, precision=HIGH).reshape(rhs_width, SUBS * OWN)
    residual = right_sides - applied
    solution = first_pass + precondition(residual, local_inverse, coarse_basis, coarse_inverse, send_index, halo_count)
    return (solution, residual)
```

```python
import functools

import jax
import jax.numpy as jnp
from jax import lax
from jax.experimental import pallas as pl
from jax.experimental.pallas import tpu as pltpu
from jax.sharding import PartitionSpec as P

MESH = pl.DeviceIdType.MESH
F32 = jnp.float32
BF16 = jnp.bfloat16


def split(x):
    hi = x.astype(BF16)
    return hi, (x - hi.astype(F32)).astype(BF16)


def mm(x, w_hi, w_lo, dims=(((1,), (0,)), ((), ()))):
    x_hi, x_lo = split(x)
    rows = x.shape[0]
    both = lax.dot_general(
        jnp.concatenate([x_hi, x_lo], axis=0), w_hi, dims, preferred_element_type=F32
    )
    low = lax.dot_general(x_hi, w_lo, dims, preferred_element_type=F32)
    return both[:rows] + (both[rows:] + low)


def kernel(
    nsub, ncol,
    rhs_hbm, op_hbm, inv_hbm, basis_hbm, cinv_hbm, index_ref, count_ref,
    sol_ref, res_ref,
    inv_f, op_f, basis_f, cinv_f,
    inv_h, inv_l, op_h, op_l, basis_h, basis_l, cinv_h, cinv_l, sel,
    xbuf, hbuf, pack, coeff, kept, coarse, mix,
    in_sem, halo_s, halo_r, field_s, field_r, kept_s, kept_r, mix_s, mix_r, coarse_s, coarse_r,
):
    s = lax.axis_index("sub")
    c = lax.axis_index("col")
    nrhs, own = xbuf.shape[2], xbuf.shape[3]
    slots = index_ref.shape[3]
    nb = index_ref.shape[2]
    halo = nb * slots
    ch = own + halo
    modes = basis_f.shape[1]
    mq = modes // ncol
    stride = nsub // 4
    offsets = (1, -1, stride, -stride)

    loads = []
    for number, (src, dst) in enumerate((
        (rhs_hbm, xbuf.at[0, c]),
        (basis_hbm.at[0], basis_f),
        (inv_hbm.at[0], inv_f),
        (cinv_hbm, cinv_f),
        (op_hbm.at[0], op_f),
    )):
        load = pltpu.make_async_copy(src, dst, in_sem.at[number])
        load.start()
        loads.append(load)

    hbuf[...] = jnp.zeros_like(hbuf)

    barrier = pltpu.get_barrier_semaphore()

    def greet(k, carry):
        pl.semaphore_signal(
            barrier, inc=1, device_id=(lax.rem(s + k, nsub), c), device_id_type=MESH
        )
        return carry

    lax.fori_loop(1, nsub, greet, 0)
    expected = nsub - 1 + ncol - 1
    for dc in range(1, ncol):
        other = lax.rem(c + dc, ncol)
        pl.semaphore_signal(barrier, inc=1, device_id=(s, other), device_id_type=MESH)
        for d in offsets:
            t = s + d

            @pl.when(jnp.logical_and(t >= 0, t < nsub))
            def _():
                pl.semaphore_signal(barrier, inc=1, device_id=(t, other), device_id_type=MESH)

            expected = expected + jnp.where(jnp.logical_and(t >= 0, t < nsub), 1, 0)

    slot = lax.broadcasted_iota(jnp.int32, (1, slots), 1)
    row = jnp.concatenate(
        [
            jnp.where(slot < count_ref[0, 0, n], index_ref[0, 0, n : n + 1, :], -1)
            for n in range(nb)
        ],
        axis=1,
    )
    place = lax.broadcasted_iota(jnp.int32, (own, halo), 0)
    sel[...] = jnp.where(place == row, 1.0, 0.0).astype(BF16)

    def pack_rows(rnd, x):
        x_hi, x_lo = split(x)
        both = jnp.dot(
            jnp.concatenate([x_hi, x_lo], axis=0), sel[...], preferred_element_type=F32
        )
        pack[rnd] = (both[:nrhs] + both[nrhs:]).T

    def halo_copy(rnd, n, dc):
        rows = pl.ds(n * slots, slots)
        return pltpu.make_async_remote_copy(
            src_ref=pack.at[rnd, rows],
            dst_ref=hbuf.at[rnd, c, rows],
            send_sem=halo_s.at[rnd, n, dc],
            recv_sem=halo_r.at[rnd, n, c],
            device_id=(s + offsets[n], lax.rem(c + dc, ncol)),
            device_id_type=MESH,
        )

    def halo_each(rnd, act):
        for n in range(nb):
            t = s + offsets[n]

            @pl.when(jnp.logical_and(t >= 0, t < nsub))
            def _():
                for dc in range(ncol):
                    act(halo_copy(rnd, n, dc))

    def halo_wait(rnd, dc):
        source = lax.rem(c + ncol - dc, ncol)
        for n in range(nb):
            t = s - offsets[n]
            rows = pl.ds(n * slots, slots)

            @pl.when(jnp.logical_and(t >= 0, t < nsub))
            def _():
                pltpu.make_async_remote_copy(
                    src_ref=pack.at[rnd, rows],
                    dst_ref=hbuf.at[rnd, source, rows],
                    send_sem=halo_s.at[rnd, n, dc],
                    recv_sem=halo_r.at[rnd, n, source],
                    device_id=(t, source),
                    device_id_type=MESH,
                ).wait_recv()

    def peer_copy(src, buf, sems_s, sems_r, dc, arriving):
        index = lax.rem(c + ncol - dc, ncol) if arriving else c
        return pltpu.make_async_remote_copy(
            src_ref=src,
            dst_ref=buf.at[index],
            send_sem=sems_s.at[dc],
            recv_sem=sems_r.at[index],
            device_id=(s, lax.rem(c + dc, ncol)),
            device_id_type=MESH,
        )

    def field_copy(rnd, dc, arriving=False):
        return peer_copy(
            xbuf.at[rnd, c], xbuf.at[rnd], field_s.at[rnd], field_r.at[rnd], dc, arriving
        )

    def coarse_copy(rnd, dc, arriving=False):
        return peer_copy(
            coarse.at[rnd, c], coarse.at[rnd], coarse_s.at[rnd], coarse_r.at[rnd], dc, arriving
        )

    def mix_copy(dc, arriving=False):
        target = pl.multiple_of(lax.rem(c + dc, ncol) * mq, mq)
        return peer_copy(
            coeff.at[1, pl.ds(target, mq)], mix, mix_s, mix_r, dc, arriving
        )

    def kept_copy(rnd, k, arriving=False):
        index = lax.rem(s + nsub - k, nsub) if arriving else s
        return pltpu.make_async_remote_copy(
            src_ref=kept.at[rnd, s],
            dst_ref=kept.at[rnd, index],
            send_sem=kept_s.at[rnd, k],
            recv_sem=kept_r.at[rnd, index],
            device_id=(lax.rem(s + k, nsub), c),
            device_id_type=MESH,
        )

    def kept_all(rnd, act):
        def step(k, carry):
            act(k)
            return carry

        lax.fori_loop(1, nsub, step, 0)

    def split_rows(src, hi, lo, rows):
        def step(i, carry):
            at = pl.ds(pl.multiple_of(i * rows, rows), rows)
            hi[at, :], lo[at, :] = split(src[at, :])
            return carry

        lax.fori_loop(0, src.shape[0] // rows, step, 0)

    def block_rows(b):
        return pl.ds(pl.multiple_of(b * ch, 128), own)

    def halo_rows(b):
        return pl.ds(pl.multiple_of(b * ch + own, 128), halo)

    def ext_block(rnd, b):
        return jnp.concatenate([xbuf[rnd, b], hbuf[rnd, b].T], axis=1)

    def all_rows(b):
        return pl.ds(pl.multiple_of(b * ch, 128), ch)

    def coarse_sum(rnd):
        mine = pl.ds(pl.multiple_of(c * mq, mq), mq)
        kept_all(rnd, lambda k: kept_copy(rnd, k).start())
        return mine

    def coarse_solve(rnd):
        kept_all(rnd, lambda k: kept_copy(rnd, k, True).wait_recv())
        k_hi, k_lo = split(kept[rnd].reshape(nsub * mq, nrhs))
        part = jnp.dot(cinv_h[...], k_hi, preferred_element_type=F32)
        part += jnp.dot(cinv_l[...], k_hi, preferred_element_type=F32)
        part += jnp.dot(cinv_h[...], k_lo, preferred_element_type=F32)
        coarse[rnd, c] = part
        for dc in range(1, ncol):
            coarse_copy(rnd, dc).start()

    def coarse_values(rnd):
        for dc in range(1, ncol):
            coarse_copy(rnd, dc, True).wait_recv()
        return jnp.sum(coarse[rnd], axis=0).T

    def coarse_part(values, b):
        rows = block_rows(b)
        return mm(values, basis_h[rows, :], basis_l[rows, :], (((1,), (1,)), ((), ())))

    loads[0].wait()
    pack_rows(0, xbuf[0, c])
    pl.semaphore_wait(barrier, expected)
    halo_each(0, lambda copy: copy.start())
    for dc in range(1, ncol):
        field_copy(0, dc).start()
    loads[1].wait()
    split_rows(basis_f, basis_h, basis_l, 128)
    loads[2].wait()
    split_rows(inv_f, inv_h, inv_l, 128)
    loads[3].wait()
    cinv_h[...], cinv_l[...] = split(cinv_f[...])
    for dc in range(ncol):
        halo_wait(0, dc)
    for dc in range(1, ncol):
        field_copy(0, dc, True).wait_recv()

    mine = pl.ds(pl.multiple_of(c * mq, mq), mq)
    amount = jnp.zeros((nrhs, modes), F32)
    for b in range(ncol):
        rows = all_rows(b)
        amount += mm(ext_block(0, b), basis_h[rows, :], basis_l[rows, :])
    coeff[0] = amount.T
    kept[0, s] = coeff[0, mine, :]
    kept_all(0, lambda k: kept_copy(0, k).start())

    local = jnp.zeros((nrhs, own), F32)
    for b in range(ncol):
        rows = all_rows(b)
        local += mm(ext_block(0, b), inv_h[rows, :], inv_l[rows, :])
    xbuf[1, c] = local
    for dc in range(1, ncol):
        field_copy(1, dc).start()
    loads[4].wait()
    split_rows(op_f, op_h, op_l, 128)

    coarse_solve(0)
    values = coarse_values(0)
    sol_ref[...] = xbuf[1, c] + coarse_part(values, c)
    pack_rows(1, sol_ref[...])
    halo_each(1, lambda copy: copy.start())

    for dc in range(1, ncol):
        field_copy(1, dc, True).wait_recv()
    applied = jnp.zeros((nrhs, own), F32)
    for b in range(ncol):
        rows = block_rows(b)
        applied += mm(
            xbuf[1, b] + coarse_part(values, b), op_h[rows, :], op_l[rows, :]
        )
    for dc in range(ncol):
        halo_wait(1, dc)
    for b in range(ncol):
        rows = halo_rows(b)
        applied += mm(hbuf[1, b].T, op_h[rows, :], op_l[rows, :])
    residual = xbuf[0, c] - applied
    res_ref[...] = residual
    xbuf[2, c] = residual
    pack_rows(2, residual)
    halo_each(2, lambda copy: copy.start())

    rows = block_rows(c)
    amount = mm(xbuf[2, c], basis_h[rows, :], basis_l[rows, :])
    halo_wait(2, 0)
    rows = halo_rows(c)
    amount += mm(hbuf[2, c].T, basis_h[rows, :], basis_l[rows, :])
    coeff[1] = amount.T
    for dc in range(1, ncol):
        mix_copy(dc).start()
    for dc in range(1, ncol):
        field_copy(2, dc).start()
    total = coeff[1, mine, :]
    for dc in range(1, ncol):
        mix_copy(dc, True).wait_recv()
        total += mix[lax.rem(c + ncol - dc, ncol)]
    kept[1, s] = total
    kept_all(1, lambda k: kept_copy(1, k).start())

    rows = all_rows(c)
    sol_ref[...] += mm(ext_block(2, c), inv_h[rows, :], inv_l[rows, :])
    for dc in range(1, ncol):
        b = lax.rem(c + ncol - dc, ncol)
        halo_wait(2, dc)
        field_copy(2, dc, True).wait_recv()
        rows = all_rows(b)
        sol_ref[...] += mm(ext_block(2, b), inv_h[rows, :], inv_l[rows, :])
    coarse_solve(1)
    sol_ref[...] += coarse_part(coarse_values(1), c)

    for rnd in range(3):
        halo_each(rnd, lambda copy: copy.wait_send())
        for dc in range(1, ncol):
            field_copy(rnd, dc).wait_send()
    for rnd in range(2):
        kept_all(rnd, lambda k: kept_copy(rnd, k).wait_send())
        for dc in range(1, ncol):
            coarse_copy(rnd, dc).wait_send()
    for dc in range(1, ncol):
        mix_copy(dc).wait_send()


def body(
    nsub, ncol,
    right_sides, operator, local_inverse, coarse_basis, coarse_inverse, send_index, halo_count,
):
    nrhs, own = right_sides.shape
    _, ext, modes = coarse_basis.shape
    nb, slots = send_index.shape[2:]
    halo = nb * slots
    mq = modes // ncol
    kept_rows = coarse_inverse.shape[1]
    dma = pltpu.SemaphoreType.DMA
    any_spec = pl.BlockSpec(memory_space=pl.ANY)
    vmem = pl.BlockSpec(memory_space=pltpu.VMEM)
    out = jax.ShapeDtypeStruct((nrhs, own), F32)
    return pl.pallas_call(
        functools.partial(kernel, nsub, ncol),
        out_shape=(out, out),
        in_specs=[any_spec] * 5 + [vmem, pl.BlockSpec(memory_space=pltpu.SMEM)],
        out_specs=(vmem, vmem),
        scratch_shapes=[
            pltpu.VMEM((ext, own), F32),
            pltpu.VMEM((ext, own), F32),
            pltpu.VMEM((ext, modes), F32),
            pltpu.VMEM((modes, kept_rows), F32),
            pltpu.VMEM((ext, own), BF16),
            pltpu.VMEM((ext, own), BF16),
            pltpu.VMEM((ext, own), BF16),
            pltpu.VMEM((ext, own), BF16),
            pltpu.VMEM((ext, modes), BF16),
            pltpu.VMEM((ext, modes), BF16),
            pltpu.VMEM((modes, kept_rows), BF16),
            pltpu.VMEM((modes, kept_rows), BF16),
            pltpu.VMEM((own, halo), BF16),
            pltpu.VMEM((3, ncol, nrhs, own), F32),
            pltpu.VMEM((3, ncol, halo, nrhs), F32),
            pltpu.VMEM((3, halo, nrhs), F32),
            pltpu.VMEM((2, modes, nrhs), F32),
            pltpu.VMEM((2, nsub, mq, nrhs), F32),
            pltpu.VMEM((2, ncol, modes, nrhs), F32),
            pltpu.VMEM((ncol, mq, nrhs), F32),
            dma((5,)),
            dma((3, nb, ncol)),
            dma((3, nb, ncol)),
            dma((3, ncol)),
            dma((3, ncol)),
            dma((2, nsub)),
            dma((2, nsub)),
            dma((ncol,)),
            dma((ncol,)),
            dma((2, ncol)),
            dma((2, ncol)),
        ],
        compiler_params=pltpu.CompilerParams(
            collective_id=0, has_side_effects=True, vmem_limit_bytes=48 * 1024 * 1024
        ),
    )(right_sides, operator, local_inverse, coarse_basis, coarse_inverse, send_index, halo_count)


def solution(mesh):
    placed = (
        P(None, ("sub", "col")),
        P("sub", None, "col"),
        P("sub", None, "col"),
        P("sub", None, None),
        P("sub", "col"),
        P("sub", "col", None, None),
        P("sub", "col", None),
    )
    return jax.shard_map(
        functools.partial(body, mesh.shape["sub"], mesh.shape["col"]),
        mesh=mesh,
        in_specs=placed,
        out_specs=(P(None, ("sub", "col")), P(None, ("sub", "col"))),
        check_vma=False,
    )
```

```python
import functools

import jax
import jax.numpy as jnp
from jax import lax
from jax.experimental import pallas as pl
from jax.experimental.pallas import tpu as pltpu
from jax.sharding import PartitionSpec as P

TRANS = (((1,), (1,)), ((), ()))
MESH = pl.DeviceIdType.MESH
F32 = jnp.float32
BF16 = jnp.bfloat16


def split(x):
    hi = x.astype(BF16)
    return hi, (x - hi.astype(F32)).astype(BF16)


def mm(x, w_hi, w_lo, dims=(((1,), (0,)), ((), ()))):
    x_hi, x_lo = split(x)
    rows = x.shape[0]
    both = lax.dot_general(
        jnp.concatenate([x_hi, x_lo], axis=0), w_hi, dims, preferred_element_type=F32
    )
    low = lax.dot_general(x_hi, w_lo, dims, preferred_element_type=F32)
    return both[:rows] + (both[rows:] + low)


def fold(x):
    half = x.shape[0] // 2
    return jnp.concatenate([x[:half], x[half:]], axis=1)


def unfold(x):
    width = x.shape[-1] // 2
    return jnp.concatenate([x[..., :width], x[..., width:]], axis=-2)


def kernel(
    nsub, ncol,
    rhs_hbm, op_hbm, inv_hbm, basis_hbm, cinv_hbm, index_hbm, count_hbm,
    sol_ref, res_ref,
    index_ref, count_ref, inv_f, op_f, basis_f, cinv_f,
    inv_h, inv_l, op_h, op_l, basis_h, basis_l, cinv_h, cinv_l, sel,
    xbuf, hbuf, pack, coeff, kept, coarse, mix,
    in_sem, halo_s, halo_r, field_s, field_r, kept_s, kept_r, mix_s, mix_r, coarse_s, coarse_r,
):
    s = lax.axis_index("sub")
    c = lax.axis_index("col")
    nrhs, own = xbuf.shape[2], xbuf.shape[3]
    slots = index_ref.shape[3]
    nb = index_ref.shape[2]
    halo = nb * slots
    ch = own + halo
    modes = basis_f.shape[0]
    mq = modes // ncol
    stride = nsub // 4
    offsets = (1, -1, stride, -stride)

    loads = []
    for number, (src, dst) in enumerate((
        (index_hbm, index_ref),
        (count_hbm, count_ref),
        (rhs_hbm, xbuf.at[0, c]),
        (basis_hbm.at[0], basis_f),
        (inv_hbm.at[0], inv_f),
        (cinv_hbm, cinv_f),
        (op_hbm.at[0], op_f),
    )):
        load = pltpu.make_async_copy(src, dst, in_sem.at[number])
        load.start()
        loads.append(load)

    hbuf[...] = jnp.zeros_like(hbuf)

    barrier = pltpu.get_barrier_semaphore()

    def greet(k, carry):
        pl.semaphore_signal(
            barrier, inc=1, device_id=(lax.rem(s + k, nsub), c), device_id_type=MESH
        )
        return carry

    lax.fori_loop(1, nsub, greet, 0)
    expected = nsub - 1 + ncol - 1
    for dc in range(1, ncol):
        other = lax.rem(c + dc, ncol)
        pl.semaphore_signal(barrier, inc=1, device_id=(s, other), device_id_type=MESH)
        for d in offsets:
            t = s + d

            @pl.when(jnp.logical_and(t >= 0, t < nsub))
            def _():
                pl.semaphore_signal(barrier, inc=1, device_id=(t, other), device_id_type=MESH)

            expected = expected + jnp.where(jnp.logical_and(t >= 0, t < nsub), 1, 0)

    loads[0].wait()
    loads[1].wait()
    slot = lax.broadcasted_iota(jnp.int32, (1, slots), 1)
    row = jnp.concatenate(
        [
            jnp.where(slot < count_ref[0, 0, n], index_ref[0, 0, n : n + 1, :], -1)
            for n in range(nb)
        ],
        axis=1,
    )
    place = lax.broadcasted_iota(jnp.int32, (own, halo), 0)
    sel[...] = jnp.where(place == row, 1.0, 0.0).astype(BF16)

    def pack_rows(rnd, x):
        x_hi, x_lo = split(x)
        both = jnp.dot(
            jnp.concatenate([x_hi, x_lo], axis=0), sel[...], preferred_element_type=F32
        )
        rows = (both[:nrhs] + both[nrhs:]).T
        for n in range(nb):
            pack[rnd, n] = fold(rows[n * slots : (n + 1) * slots])

    def halo_copy(rnd, n, dc):
        return pltpu.make_async_remote_copy(
            src_ref=pack.at[rnd, n],
            dst_ref=hbuf.at[rnd, c, n],
            send_sem=halo_s.at[rnd, n, dc],
            recv_sem=halo_r.at[rnd, n, c],
            device_id=(s + offsets[n], lax.rem(c + dc, ncol)),
            device_id_type=MESH,
        )

    def halo_each(rnd, act):
        for n in range(nb):
            t = s + offsets[n]

            @pl.when(jnp.logical_and(t >= 0, t < nsub))
            def _():
                for dc in range(ncol):
                    act(halo_copy(rnd, n, dc))

    def halo_wait(rnd, dc):
        source = lax.rem(c + ncol - dc, ncol)
        for n in range(nb):
            t = s - offsets[n]

            @pl.when(jnp.logical_and(t >= 0, t < nsub))
            def _():
                pltpu.make_async_remote_copy(
                    src_ref=pack.at[rnd, n],
                    dst_ref=hbuf.at[rnd, source, n],
                    send_sem=halo_s.at[rnd, n, dc],
                    recv_sem=halo_r.at[rnd, n, source],
                    device_id=(t, source),
                    device_id_type=MESH,
                ).wait_recv()

    def peer_copy(src, buf, sems_s, sems_r, dc, arriving):
        index = lax.rem(c + ncol - dc, ncol) if arriving else c
        return pltpu.make_async_remote_copy(
            src_ref=src,
            dst_ref=buf.at[index],
            send_sem=sems_s.at[dc],
            recv_sem=sems_r.at[index],
            device_id=(s, lax.rem(c + dc, ncol)),
            device_id_type=MESH,
        )

    def field_copy(rnd, dc, arriving=False):
        return peer_copy(
            xbuf.at[rnd, c], xbuf.at[rnd], field_s.at[rnd], field_r.at[rnd], dc, arriving
        )

    def coarse_copy(rnd, dc, arriving=False):
        return peer_copy(
            coarse.at[rnd, c], coarse.at[rnd], coarse_s.at[rnd], coarse_r.at[rnd], dc, arriving
        )

    def mix_copy(dc, arriving=False):
        return peer_copy(
            coeff.at[lax.rem(c + dc, ncol)], mix, mix_s, mix_r, dc, arriving
        )

    def kept_copy(rnd, k, arriving=False):
        index = lax.rem(s + nsub - k, nsub) if arriving else s
        return pltpu.make_async_remote_copy(
            src_ref=kept.at[rnd, s],
            dst_ref=kept.at[rnd, index],
            send_sem=kept_s.at[rnd, k],
            recv_sem=kept_r.at[rnd, index],
            device_id=(lax.rem(s + k, nsub), c),
            device_id_type=MESH,
        )

    def kept_all(rnd, act):
        def step(k, carry):
            act(k)
            return carry

        lax.fori_loop(1, nsub, step, 0)

    def split_rows(src, hi, lo, rows):
        def step(i, carry):
            at = pl.ds(pl.multiple_of(i * rows, rows), rows)
            hi[at, :], lo[at, :] = split(src[at, :])
            return carry

        lax.fori_loop(0, src.shape[0] // rows, step, 0)

    def block_rows(b):
        return pl.ds(pl.multiple_of(b * ch, 128), own)

    def halo_rows(b):
        return pl.ds(pl.multiple_of(b * ch + own, 128), halo)

    def ext_block(rnd, b):
        return jnp.concatenate([xbuf[rnd, b], halo_field(rnd, b)], axis=1)

    def all_rows(b):
        return pl.ds(pl.multiple_of(b * ch, 128), ch)

    def halo_field(rnd, b):
        return unfold(hbuf[rnd, b]).reshape(halo, nrhs).T

    def coarse_solve(rnd):
        kept_all(rnd, lambda k: kept_copy(rnd, k, True).wait_recv())
        k_hi, k_lo = split(unfold(kept[rnd]).reshape(nsub * mq, nrhs))
        part = jnp.dot(cinv_h[...], k_hi, preferred_element_type=F32)
        part += jnp.dot(cinv_l[...], k_hi, preferred_element_type=F32)
        part += jnp.dot(cinv_h[...], k_lo, preferred_element_type=F32)
        coarse[rnd, c] = fold(part)
        for dc in range(1, ncol):
            coarse_copy(rnd, dc).start()

    def coarse_values(rnd):
        for dc in range(1, ncol):
            coarse_copy(rnd, dc, True).wait_recv()
        return unfold(jnp.sum(coarse[rnd], axis=0)).T

    def coarse_part(values, b):
        rows = block_rows(b)
        return mm(values, basis_h[:, rows], basis_l[:, rows])

    def set_coeff(amount):
        rows = amount.T
        for b in range(ncol):
            coeff[b] = fold(rows[b * mq : (b + 1) * mq])

    loads[2].wait()
    pack_rows(0, xbuf[0, c])
    pl.semaphore_wait(barrier, expected)
    halo_each(0, lambda copy: copy.start())
    for dc in range(1, ncol):
        field_copy(0, dc).start()
    loads[3].wait()
    basis_h[...], basis_l[...] = split(basis_f[...])
    loads[4].wait()
    split_rows(inv_f, inv_h, inv_l, 128)
    loads[5].wait()
    cinv_h[...], cinv_l[...] = split(cinv_f[...])
    for dc in range(ncol):
        halo_wait(0, dc)
    for dc in range(1, ncol):
        field_copy(0, dc, True).wait_recv()

    amount = jnp.zeros((nrhs, modes), F32)
    for b in range(ncol):
        rows = all_rows(b)
        amount += mm(ext_block(0, b), basis_h[:, rows], basis_l[:, rows], TRANS)
    set_coeff(amount)
    kept[0, s] = coeff[c]
    kept_all(0, lambda k: kept_copy(0, k).start())

    local = jnp.zeros((nrhs, own), F32)
    for b in range(ncol):
        rows = all_rows(b)
        local += mm(ext_block(0, b), inv_h[rows, :], inv_l[rows, :])
    xbuf[1, c] = local
    for dc in range(1, ncol):
        field_copy(1, dc).start()
    loads[6].wait()
    split_rows(op_f, op_h, op_l, 128)

    coarse_solve(0)
    values = coarse_values(0)
    sol_ref[...] = xbuf[1, c] + coarse_part(values, c)
    pack_rows(1, sol_ref[...])
    halo_each(1, lambda copy: copy.start())

    for dc in range(1, ncol):
        field_copy(1, dc, True).wait_recv()
    applied = jnp.zeros((nrhs, own), F32)
    for b in range(ncol):
        rows = block_rows(b)
        applied += mm(
            xbuf[1, b] + coarse_part(values, b), op_h[rows, :], op_l[rows, :]
        )
    for dc in range(ncol):
        halo_wait(1, dc)
    for b in range(ncol):
        rows = halo_rows(b)
        applied += mm(halo_field(1, b), op_h[rows, :], op_l[rows, :])
    residual = xbuf[0, c] - applied
    res_ref[...] = residual
    xbuf[2, c] = residual
    pack_rows(2, residual)
    halo_each(2, lambda copy: copy.start())

    rows = block_rows(c)
    amount = mm(xbuf[2, c], basis_h[:, rows], basis_l[:, rows], TRANS)
    halo_wait(2, 0)
    rows = halo_rows(c)
    amount += mm(halo_field(2, c), basis_h[:, rows], basis_l[:, rows], TRANS)
    set_coeff(amount)
    for dc in range(1, ncol):
        mix_copy(dc).start()
    for dc in range(1, ncol):
        field_copy(2, dc).start()
    total = coeff[c]
    for dc in range(1, ncol):
        mix_copy(dc, True).wait_recv()
        total += mix[lax.rem(c + ncol - dc, ncol)]
    kept[1, s] = total
    kept_all(1, lambda k: kept_copy(1, k).start())

    rows = all_rows(c)
    sol_ref[...] += mm(ext_block(2, c), inv_h[rows, :], inv_l[rows, :])
    for dc in range(1, ncol):
        b = lax.rem(c + ncol - dc, ncol)
        halo_wait(2, dc)
        field_copy(2, dc, True).wait_recv()
        rows = all_rows(b)
        sol_ref[...] += mm(ext_block(2, b), inv_h[rows, :], inv_l[rows, :])
    coarse_solve(1)
    sol_ref[...] += coarse_part(coarse_values(1), c)

    for rnd in range(3):
        halo_each(rnd, lambda copy: copy.wait_send())
        for dc in range(1, ncol):
            field_copy(rnd, dc).wait_send()
    for rnd in range(2):
        kept_all(rnd, lambda k: kept_copy(rnd, k).wait_send())
        for dc in range(1, ncol):
            coarse_copy(rnd, dc).wait_send()
    for dc in range(1, ncol):
        mix_copy(dc).wait_send()


def body(
    nsub, ncol,
    right_sides, operator, local_inverse, coarse_basis, coarse_inverse, send_index, halo_count,
):
    nrhs, own = right_sides.shape
    _, ext, modes = coarse_basis.shape
    nb, slots = send_index.shape[2:]
    halo = nb * slots
    mq = modes // ncol
    kept_rows = coarse_inverse.shape[1]
    dma = pltpu.SemaphoreType.DMA
    any_spec = pl.BlockSpec(memory_space=pltpu.HBM)
    vmem = pl.BlockSpec(memory_space=pltpu.VMEM)
    out = jax.ShapeDtypeStruct((nrhs, own), F32)
    return pl.pallas_call(
        functools.partial(kernel, nsub, ncol),
        out_shape=(out, out),
        in_specs=[any_spec] * 7,
        out_specs=(vmem, vmem),
        scratch_shapes=[
            pltpu.VMEM(send_index.shape, jnp.int32),
            pltpu.SMEM(halo_count.shape, jnp.int32),
            pltpu.VMEM((ext, own), F32),
            pltpu.VMEM((ext, own), F32),
            pltpu.VMEM((modes, ext), F32),
            pltpu.VMEM((modes, kept_rows), F32),
            pltpu.VMEM((ext, own), BF16),
            pltpu.VMEM((ext, own), BF16),
            pltpu.VMEM((ext, own), BF16),
            pltpu.VMEM((ext, own), BF16),
            pltpu.VMEM((modes, ext), BF16),
            pltpu.VMEM((modes, ext), BF16),
            pltpu.VMEM((modes, kept_rows), BF16),
            pltpu.VMEM((modes, kept_rows), BF16),
            pltpu.VMEM((own, halo), BF16),
            pltpu.VMEM((3, ncol, nrhs, own), F32),
            pltpu.VMEM((3, ncol, nb, slots // 2, 2 * nrhs), F32),
            pltpu.VMEM((3, nb, slots // 2, 2 * nrhs), F32),
            pltpu.VMEM((ncol, mq // 2, 2 * nrhs), F32),
            pltpu.VMEM((2, nsub, mq // 2, 2 * nrhs), F32),
            pltpu.VMEM((2, ncol, modes // 2, 2 * nrhs), F32),
            pltpu.VMEM((ncol, mq // 2, 2 * nrhs), F32),
            dma((7,)),
            dma((3, nb, ncol)),
            dma((3, nb, ncol)),
            dma((3, ncol)),
            dma((3, ncol)),
            dma((2, nsub)),
            dma((2, nsub)),
            dma((ncol,)),
            dma((ncol,)),
            dma((2, ncol)),
            dma((2, ncol)),
        ],
        compiler_params=pltpu.CompilerParams(
            collective_id=0, has_side_effects=True, vmem_limit_bytes=56 * 1024 * 1024
        ),
    )(
        right_sides, operator, local_inverse, jnp.swapaxes(coarse_basis, 1, 2),
        coarse_inverse, send_index, halo_count,
    )


def solution(mesh):
    placed = (
        P(None, ("sub", "col")),
        P("sub", None, "col"),
        P("sub", None, "col"),
        P("sub", None, None),
        P("sub", "col"),
        P("sub", "col", None, None),
        P("sub", "col", None),
    )
    return jax.shard_map(
        functools.partial(body, mesh.shape["sub"], mesh.shape["col"]),
        mesh=mesh,
        in_specs=placed,
        out_specs=(P(None, ("sub", "col")), P(None, ("sub", "col"))),
        check_vma=False,
    )
```

```python
import functools

import jax
import jax.numpy as jnp
from jax import lax
from jax.experimental import pallas as pl
from jax.experimental.pallas import tpu as pltpu
from jax.sharding import PartitionSpec as P

TRANS = (((1,), (1,)), ((), ()))
MESH = pl.DeviceIdType.MESH
F32 = jnp.float32
BF16 = jnp.bfloat16


def split(x):
    hi = x.astype(BF16)
    return hi, (x - hi.astype(F32)).astype(BF16)


def mm(x, w_hi, w_lo, dims=(((1,), (0,)), ((), ()))):
    x_hi, x_lo = split(x)
    rows = x.shape[0]
    both = lax.dot_general(
        jnp.concatenate([x_hi, x_lo], axis=0), w_hi, dims, preferred_element_type=F32
    )
    low = lax.dot_general(x_hi, w_lo, dims, preferred_element_type=F32)
    return both[:rows] + (both[rows:] + low)


def fold(x):
    half = x.shape[0] // 2
    return jnp.concatenate([x[:half], x[half:]], axis=1)


def unfold(x):
    width = x.shape[-1] // 2
    return jnp.concatenate([x[..., :width], x[..., width:]], axis=-2)


def kernel(
    nsub, ncol,
    rhs_hbm, op_hbm, inv_hbm, basis_hbm, cinv_hbm, index_hbm, count_hbm,
    sol_ref, res_ref,
    index_ref, count_ref, inv_f, op_f, basis_f, cinv_f,
    inv_h, inv_l, op_h, op_l, basis_h, basis_l, cinv_h, cinv_l, sel,
    xbuf, hbuf, pack, coeff, kept, coarse, mix, nco, near, parts, cbuf,
    in_sem, halo_s, halo_r, field_s, field_r, kept_s, kept_r, mix_s, mix_r, coarse_s, coarse_r,
    nco_s, nco_r, near_s, near_r, part_s, part_r,
):
    s = lax.axis_index("sub")
    c = lax.axis_index("col")
    nrhs, own = xbuf.shape[2], xbuf.shape[3]
    slots = index_ref.shape[3]
    nb = index_ref.shape[2]
    halo = nb * slots
    ch = own + halo
    modes = basis_f.shape[0]
    mq = modes // ncol
    stride = nsub // 4
    offsets = (1, -1, stride, -stride)

    loads = []
    for number, (src, dst) in enumerate((
        (index_hbm, index_ref),
        (count_hbm, count_ref),
        (rhs_hbm, xbuf.at[0, c]),
        (basis_hbm.at[0], basis_f),
        (inv_hbm.at[0], inv_f),
        (cinv_hbm, cinv_f),
        (op_hbm.at[0], op_f),
    )):
        load = pltpu.make_async_copy(src, dst, in_sem.at[number])
        load.start()
        loads.append(load)

    hbuf[...] = jnp.zeros_like(hbuf)
    nco[...] = jnp.zeros_like(nco)
    cbuf[...] = jnp.zeros_like(cbuf)
    near[...] = jnp.zeros_like(near)

    barrier = pltpu.get_barrier_semaphore()

    def greet(k, carry):
        pl.semaphore_signal(
            barrier, inc=1, device_id=(lax.rem(s + k, nsub), c), device_id_type=MESH
        )
        return carry

    lax.fori_loop(1, nsub, greet, 0)
    expected = nsub - 1 + ncol - 1
    for dc in range(1, ncol):
        other = lax.rem(c + dc, ncol)
        pl.semaphore_signal(barrier, inc=1, device_id=(s, other), device_id_type=MESH)
        for d in offsets:
            t = s + d

            @pl.when(jnp.logical_and(t >= 0, t < nsub))
            def _():
                pl.semaphore_signal(barrier, inc=1, device_id=(t, other), device_id_type=MESH)

            expected = expected + jnp.where(jnp.logical_and(t >= 0, t < nsub), 1, 0)

    loads[0].wait()
    loads[1].wait()
    slot = lax.broadcasted_iota(jnp.int32, (1, slots), 1)
    row = jnp.concatenate(
        [
            jnp.where(slot < count_ref[0, 0, n], index_ref[0, 0, n : n + 1, :], -1)
            for n in range(nb)
        ],
        axis=1,
    )
    place = lax.broadcasted_iota(jnp.int32, (own, halo), 0)
    sel[...] = jnp.where(place == row, 1.0, 0.0).astype(BF16)

    def pack_rows(rnd, x):
        x_hi, x_lo = split(x)
        both = jnp.dot(
            jnp.concatenate([x_hi, x_lo], axis=0), sel[...], preferred_element_type=F32
        )
        rows = (both[:nrhs] + both[nrhs:]).T
        for n in range(nb):
            pack[rnd, n] = fold(rows[n * slots : (n + 1) * slots])
        return rows

    def in_range(t):
        return jnp.logical_and(t >= 0, t < nsub)

    def near_copy(src, buf, sems_s, sems_r, n, dc, arriving=False):
        index = lax.rem(c + ncol - dc, ncol) if arriving else c
        t = s - offsets[n] if arriving else s + offsets[n]
        return pltpu.make_async_remote_copy(
            src_ref=src,
            dst_ref=buf.at[index, n],
            send_sem=sems_s.at[n, dc],
            recv_sem=sems_r.at[n, index],
            device_id=(t, lax.rem(c + dc, ncol)),
            device_id_type=MESH,
        )

    def near_send(make, act):
        for n in range(nb):

            @pl.when(in_range(s + offsets[n]))
            def _():
                for dc in range(ncol):
                    act(make(n, dc, False))

    def near_wait(make, dc):
        for n in range(nb):

            @pl.when(in_range(s - offsets[n]))
            def _():
                make(n, dc, True).wait_recv()

    def halo_copy(rnd):
        return lambda n, dc, arriving: near_copy(
            pack.at[rnd, n], hbuf.at[rnd], halo_s.at[rnd], halo_r.at[rnd], n, dc, arriving
        )

    def halo_each(rnd, act):
        near_send(halo_copy(rnd), act)

    def halo_wait(rnd, dc):
        near_wait(halo_copy(rnd), dc)

    def nco_copy(n, dc, arriving):
        return near_copy(coarse.at[0, c], nco, nco_s, nco_r, n, dc, arriving)

    def part_copy(n, dc, arriving):
        return near_copy(
            parts.at[n, lax.rem(c + dc, ncol)], cbuf, part_s, part_r, n, dc, arriving
        )

    def basis_copy(n):
        return pltpu.make_async_remote_copy(
            src_ref=basis_f.at[:, pl.ds(pl.multiple_of(c * ch + own, 128), halo)],
            dst_ref=near.at[n],
            send_sem=near_s.at[n],
            recv_sem=near_r.at[n],
            device_id=(s - offsets[n], c),
            device_id_type=MESH,
        )

    def peer_copy(src, buf, sems_s, sems_r, dc, arriving):
        index = lax.rem(c + ncol - dc, ncol) if arriving else c
        return pltpu.make_async_remote_copy(
            src_ref=src,
            dst_ref=buf.at[index],
            send_sem=sems_s.at[dc],
            recv_sem=sems_r.at[index],
            device_id=(s, lax.rem(c + dc, ncol)),
            device_id_type=MESH,
        )

    def field_copy(rnd, dc, arriving=False):
        return peer_copy(
            xbuf.at[rnd, c], xbuf.at[rnd], field_s.at[rnd], field_r.at[rnd], dc, arriving
        )

    def coarse_copy(rnd, dc, arriving=False):
        return peer_copy(
            coarse.at[rnd, c], coarse.at[rnd], coarse_s.at[rnd], coarse_r.at[rnd], dc, arriving
        )

    def mix_copy(dc, arriving=False):
        return peer_copy(
            coeff.at[lax.rem(c + dc, ncol)], mix, mix_s, mix_r, dc, arriving
        )

    def kept_copy(rnd, k, arriving=False):
        index = lax.rem(s + nsub - k, nsub) if arriving else s
        return pltpu.make_async_remote_copy(
            src_ref=kept.at[rnd, s],
            dst_ref=kept.at[rnd, index],
            send_sem=kept_s.at[rnd, k],
            recv_sem=kept_r.at[rnd, index],
            device_id=(lax.rem(s + k, nsub), c),
            device_id_type=MESH,
        )

    def kept_all(rnd, act):
        def step(k, carry):
            act(k)
            return carry

        lax.fori_loop(1, nsub, step, 0)

    def split_rows(src, hi, lo, rows):
        def step(i, carry):
            at = pl.ds(pl.multiple_of(i * rows, rows), rows)
            hi[at, :], lo[at, :] = split(src[at, :])
            return carry

        lax.fori_loop(0, src.shape[0] // rows, step, 0)

    def block_rows(b):
        return pl.ds(pl.multiple_of(b * ch, 128), own)

    def halo_rows(b):
        return pl.ds(pl.multiple_of(b * ch + own, 128), halo)

    def ext_block(rnd, b):
        return jnp.concatenate([xbuf[rnd, b], halo_field(rnd, b)], axis=1)

    def all_rows(b):
        return pl.ds(pl.multiple_of(b * ch, 128), ch)

    def halo_field(rnd, b):
        return unfold(hbuf[rnd, b]).reshape(halo, nrhs).T

    def coarse_solve(rnd):
        kept_all(rnd, lambda k: kept_copy(rnd, k, True).wait_recv())
        k_hi, k_lo = split(unfold(kept[rnd]).reshape(nsub * mq, nrhs))
        part = jnp.dot(cinv_h[...], k_hi, preferred_element_type=F32)
        part += jnp.dot(cinv_l[...], k_hi, preferred_element_type=F32)
        part += jnp.dot(cinv_h[...], k_lo, preferred_element_type=F32)
        coarse[rnd, c] = fold(part)
        for dc in range(1, ncol):
            coarse_copy(rnd, dc).start()
        if rnd == 0:
            near_send(nco_copy, lambda copy: copy.start())

    def coarse_values(rnd):
        for dc in range(1, ncol):
            coarse_copy(rnd, dc, True).wait_recv()
        return unfold(jnp.sum(coarse[rnd], axis=0)).T

    def coarse_part(values, b):
        rows = block_rows(b)
        return mm(values, basis_h[:, rows], basis_l[:, rows])

    def set_coeff(amount):
        rows = amount.T
        for b in range(ncol):
            coeff[b] = fold(rows[b * mq : (b + 1) * mq])

    loads[2].wait()
    pack_rows(0, xbuf[0, c])
    pl.semaphore_wait(barrier, expected)
    halo_each(0, lambda copy: copy.start())
    for dc in range(1, ncol):
        field_copy(0, dc).start()
    loads[3].wait()
    for n in range(nb):

        @pl.when(in_range(s - offsets[n]))
        def _():
            basis_copy(n).start()

    basis_h[...], basis_l[...] = split(basis_f[...])
    pack_rows(3, basis_f[:, block_rows(c)])
    halo_each(3, lambda copy: copy.start())
    loads[4].wait()
    split_rows(inv_f, inv_h, inv_l, 128)
    loads[5].wait()
    cinv_h[...], cinv_l[...] = split(cinv_f[...])
    for dc in range(ncol):
        halo_wait(0, dc)
    for dc in range(1, ncol):
        field_copy(0, dc, True).wait_recv()

    amount = jnp.zeros((nrhs, modes), F32)
    for b in range(ncol):
        rows = all_rows(b)
        amount += mm(ext_block(0, b), basis_h[:, rows], basis_l[:, rows], TRANS)
    set_coeff(amount)
    kept[0, s] = coeff[c]
    kept_all(0, lambda k: kept_copy(0, k).start())

    local = jnp.zeros((nrhs, own), F32)
    for b in range(ncol):
        rows = all_rows(b)
        local += mm(ext_block(0, b), inv_h[rows, :], inv_l[rows, :])
    xbuf[1, c] = local
    pack_rows(1, local)
    halo_each(1, lambda copy: copy.start())
    for dc in range(1, ncol):
        field_copy(1, dc).start()
    loads[6].wait()
    split_rows(op_f, op_h, op_l, 128)

    coarse_solve(0)
    values = coarse_values(0)
    sol_ref[...] = xbuf[1, c] + coarse_part(values, c)

    for dc in range(1, ncol):
        field_copy(1, dc, True).wait_recv()
    applied = jnp.zeros((nrhs, own), F32)
    for b in range(ncol):
        rows = block_rows(b)
        applied += mm(
            xbuf[1, b] + coarse_part(values, b), op_h[rows, :], op_l[rows, :]
        )
    for dc in range(ncol):
        halo_wait(1, dc)
        halo_wait(3, dc)
        near_wait(nco_copy, dc)
    added = []
    for n in range(nb):
        near_hi, near_lo = split(unfold(jnp.sum(nco[:, n], axis=0)))
        picked = unfold(hbuf[3, :, n]).reshape(ncol * slots, modes)
        added.append(mm(picked, near_hi, near_lo))
    for b in range(ncol):
        rows = halo_rows(b)
        part = jnp.concatenate([x[b * slots : (b + 1) * slots] for x in added], axis=0)
        applied += mm(halo_field(1, b) + part.T, op_h[rows, :], op_l[rows, :])
    residual = xbuf[0, c] - applied
    res_ref[...] = residual
    xbuf[2, c] = residual
    rows = pack_rows(2, residual)

    for n in range(nb):

        @pl.when(in_range(s + offsets[n]))
        def _():
            basis_wait = pltpu.make_async_remote_copy(
                src_ref=near.at[n],
                dst_ref=near.at[n],
                send_sem=near_s.at[n],
                recv_sem=near_r.at[n],
                device_id=(s + offsets[n], c),
                device_id_type=MESH,
            )
            basis_wait.wait_recv()

    for n in range(nb):
        cut = slice(n * slots, (n + 1) * slots)
        row_hi, row_lo = split(rows[cut])
        share = mm(near[n][:, cut], row_hi, row_lo)
        for b in range(ncol):
            parts[n, b] = fold(share[b * mq : (b + 1) * mq])
    near_send(part_copy, lambda copy: copy.start())
    rows = block_rows(c)
    amount = mm(residual, basis_h[:, rows], basis_l[:, rows], TRANS)
    set_coeff(amount)
    for dc in range(1, ncol):
        mix_copy(dc).start()
    halo_each(2, lambda copy: copy.start())
    for dc in range(1, ncol):
        field_copy(2, dc).start()
    total = coeff[c]
    for dc in range(1, ncol):
        mix_copy(dc, True).wait_recv()
        total += mix[lax.rem(c + ncol - dc, ncol)]
    for dc in range(ncol):
        near_wait(part_copy, dc)
    kept[1, s] = total + jnp.sum(cbuf[...], axis=(0, 1))
    kept_all(1, lambda k: kept_copy(1, k).start())

    halo_wait(2, 0)
    rows = all_rows(c)
    sol_ref[...] += mm(ext_block(2, c), inv_h[rows, :], inv_l[rows, :])
    for dc in range(1, ncol):
        b = lax.rem(c + ncol - dc, ncol)
        halo_wait(2, dc)
        field_copy(2, dc, True).wait_recv()
        rows = all_rows(b)
        sol_ref[...] += mm(ext_block(2, b), inv_h[rows, :], inv_l[rows, :])
    coarse_solve(1)
    sol_ref[...] += coarse_part(coarse_values(1), c)

    for rnd in range(4):
        halo_each(rnd, lambda copy: copy.wait_send())
    near_send(nco_copy, lambda copy: copy.wait_send())
    near_send(part_copy, lambda copy: copy.wait_send())
    for n in range(nb):

        @pl.when(in_range(s - offsets[n]))
        def _():
            basis_copy(n).wait_send()

    for rnd in range(3):
        for dc in range(1, ncol):
            field_copy(rnd, dc).wait_send()
    for rnd in range(2):
        kept_all(rnd, lambda k: kept_copy(rnd, k).wait_send())
        for dc in range(1, ncol):
            coarse_copy(rnd, dc).wait_send()
    for dc in range(1, ncol):
        mix_copy(dc).wait_send()


def body(
    nsub, ncol,
    right_sides, operator, local_inverse, coarse_basis, coarse_inverse, send_index, halo_count,
):
    nrhs, own = right_sides.shape
    _, ext, modes = coarse_basis.shape
    nb, slots = send_index.shape[2:]
    halo = nb * slots
    mq = modes // ncol
    kept_rows = coarse_inverse.shape[1]
    dma = pltpu.SemaphoreType.DMA
    any_spec = pl.BlockSpec(memory_space=pltpu.HBM)
    vmem = pl.BlockSpec(memory_space=pltpu.VMEM)
    out = jax.ShapeDtypeStruct((nrhs, own), F32)
    return pl.pallas_call(
        functools.partial(kernel, nsub, ncol),
        out_shape=(out, out),
        in_specs=[any_spec] * 7,
        out_specs=(vmem, vmem),
        scratch_shapes=[
            pltpu.VMEM(send_index.shape, jnp.int32),
            pltpu.SMEM(halo_count.shape, jnp.int32),
            pltpu.VMEM((ext, own), F32),
            pltpu.VMEM((ext, own), F32),
            pltpu.VMEM((modes, ext), F32),
            pltpu.VMEM((modes, kept_rows), F32),
            pltpu.VMEM((ext, own), BF16),
            pltpu.VMEM((ext, own), BF16),
            pltpu.VMEM((ext, own), BF16),
            pltpu.VMEM((ext, own), BF16),
            pltpu.VMEM((modes, ext), BF16),
            pltpu.VMEM((modes, ext), BF16),
            pltpu.VMEM((modes, kept_rows), BF16),
            pltpu.VMEM((modes, kept_rows), BF16),
            pltpu.VMEM((own, halo), BF16),
            pltpu.VMEM((3, ncol, nrhs, own), F32),
            pltpu.VMEM((4, ncol, nb, slots // 2, 2 * nrhs), F32),
            pltpu.VMEM((4, nb, slots // 2, 2 * nrhs), F32),
            pltpu.VMEM((ncol, mq // 2, 2 * nrhs), F32),
            pltpu.VMEM((2, nsub, mq // 2, 2 * nrhs), F32),
            pltpu.VMEM((2, ncol, modes // 2, 2 * nrhs), F32),
            pltpu.VMEM((ncol, mq // 2, 2 * nrhs), F32),
            pltpu.VMEM((ncol, nb, modes // 2, 2 * nrhs), F32),
            pltpu.VMEM((nb, modes, halo), F32),
            pltpu.VMEM((nb, ncol, mq // 2, 2 * nrhs), F32),
            pltpu.VMEM((ncol, nb, mq // 2, 2 * nrhs), F32),
            dma((7,)),
            dma((4, nb, ncol)),
            dma((4, nb, ncol)),
            dma((3, ncol)),
            dma((3, ncol)),
            dma((2, nsub)),
            dma((2, nsub)),
            dma((ncol,)),
            dma((ncol,)),
            dma((2, ncol)),
            dma((2, ncol)),
            dma((nb, ncol)),
            dma((nb, ncol)),
            dma((nb,)),
            dma((nb,)),
            dma((nb, ncol)),
            dma((nb, ncol)),
        ],
        compiler_params=pltpu.CompilerParams(
            collective_id=0, has_side_effects=True, vmem_limit_bytes=56 * 1024 * 1024
        ),
    )(
        right_sides, operator, local_inverse, jnp.swapaxes(coarse_basis, 1, 2),
        coarse_inverse, send_index, halo_count,
    )


def solution(mesh):
    placed = (
        P(None, ("sub", "col")),
        P("sub", None, "col"),
        P("sub", None, "col"),
        P("sub", None, None),
        P("sub", "col"),
        P("sub", "col", None, None),
        P("sub", "col", None),
    )
    return jax.shard_map(
        functools.partial(body, mesh.shape["sub"], mesh.shape["col"]),
        mesh=mesh,
        in_specs=placed,
        out_specs=(P(None, ("sub", "col")), P(None, ("sub", "col"))),
        check_vma=False,
    )
```
